32 devices in a mesh: groups: 2 (over x), docs: 16 (over z, y, core).
Axes of the slice: x: 2, y: 2, z: 4, core: 2. Of those that a mesh axis runs over, the one named last changes fastest.
Arguments:
- doc_acts: bfloat16 [2, 4096, 4096], P(None, ('groups', 'docs')), parts along dimension 1, may hold values from -6 to 6
- doc_grads: bfloat16 [2, 4096, 11008], P(None, ('groups', 'docs')), parts along dimension 1, may hold values from -6 to 6
- doc_segments: int32 [32, 128], P(('groups', 'docs')), parts along dimension 0, may hold values from 0 to 15, never falling along the last dimension, each value on 1 to 16 neighbouring positions
- query_acts: bfloat16 [2, 2048, 4096], P(None, ('groups', 'docs')), parts along dimension 1, may hold values from -6 to 6
- query_grads: bfloat16 [2, 2048, 11008], P(None, ('groups', 'docs')), parts along dimension 1, may hold values from -6 to 6
- query_segments: int32 [32, 64], P(('groups', 'docs')), parts along dimension 0, may hold values from 0 to 3, never falling along the last dimension, each value on 1 to 24 neighbouring positions
- input_proj: bfloat16 [4096, 64], replicated, may hold values from -0.09375 to 0.09375
- output_proj: bfloat16 [11008, 64], replicated, may hold values from -0.0546875 to 0.0546875
- step_rates: float32 [2], replicated, may hold values from 0.5 to 2
Outputs:
- scores: float32 [512, 64], P(('groups', 'docs')), parts along dimension 0
The draws below stay inside these ranges and needn't reach their ends.
There are 2 independent parts, one for each index of `groups`. The reference program is written for one: setup_inputs(seed, part) draws one part's arguments, and reference() takes and returns one part's arrays. A program takes and returns all parts, laid end to end along the dimension named above; an argument that names none is the same for every part. Nothing has to cross between parts.
Inputs may be any that keep to these rules, and one draw needn't show every extreme that they name: `doc_segments`: within each row the numbers never fall; each of the 16 documents of a row has 1 to 16 tokens, and some document has 16. `query_segments`: within each row the numbers never fall; each of the 4 queries of a row has 1 to 24 tokens, and some query has 24.
All inputs are finite; a program needn't handle non-finite values.
Results may differ from the reference program's by a relative error of at most 0.0065.
Values may be sent and summed in bfloat16 or wider, within the bound.
A program may use at most 128 MiB of HBM per device.

```python
import math
import jax
import jax.numpy as jnp
import numpy as np
from jax import lax

D = 4096
F = 11008
K = 64
CKPT = 2
TOK_DEV = 128
DOCS_DEV = 16
SEG_MOST = 16
QTOK_DEV = 64
Q_DEV = 4
TOKENS = 2048
QTOKENS = 1024
N_DOCS = 16


def block_levels(key, extent, split, low, top_value):
    factor_of, own = 1.0, jax.random.fold_in(key, 6)
    for dim, parts in split:
        heights = jnp.exp(jax.random.uniform(jax.random.fold_in(own, dim), (parts,), jnp.float32, low / len(split), top_value / len(split)))
        factor_of = factor_of * jnp.repeat(heights, extent[dim] // parts).reshape([-1 if axis == dim else 1 for axis in range(len(extent))])
    return factor_of


def split_up(amount, total, bound, lean):
    loads = [(1 << 20) // math.isqrt(grade ** lean) + 1 for grade in range(2, amount + 1)]
    rest, holding = total - bound - (amount - 1), [1] * (amount - 1)
    while rest > 0:
        movable = [i for i in range(amount - 1) if holding[i] < bound]
        mass, left = sum([loads[i] for i in movable]), rest
        for i in movable:
            more = min(bound - holding[i], max(1, left * loads[i] // mass), rest)
            holding[i] = holding[i] + more
            rest = rest - more
    return np.array([bound] + holding)


def uneven_parts(stream_key, count, total, most, lean):
    if count == 2:
        one = jax.random.randint(stream_key, (), max(1, total - most), min(most, total - 1) + 1)
        return jnp.stack([one, total - one])
    lengths = jnp.asarray(split_up(count, total, most, lean), jnp.int32)
    twos = (count - 1) // 2
    source_of, receiver = lengths[1:1 + 2 * twos:2], lengths[2:2 + 2 * twos:2]
    margin = jnp.minimum(source_of - 1, most - receiver)
    passed = jax.random.randint(jax.random.fold_in(stream_key, 1), (twos,), 0, 1 << 20) % (margin + 1)
    lengths = lengths.at[1:1 + 2 * twos:2].set(source_of - passed).at[2:2 + 2 * twos:2].set(receiver + passed)
    return lengths[jax.random.permutation(jax.random.fold_in(stream_key, 2), count)]


def bell_draw(rng, shape, scale, most, cuts=(), kind=jnp.bfloat16):
    entries = scale * jax.random.normal(rng, shape, jnp.float32)
    if cuts:
        entries = entries * block_levels(rng, shape, cuts, -0.22, 0.18)
    return jnp.clip(entries, -most, most).astype(kind)


def setup_inputs(seed: int = 0, part: int = 0) -> dict:
    key_list = jax.random.split(jax.random.key(seed), 10)
    own_keys = jax.random.split(jax.random.fold_in(key_list[9], part), 10)
    doc_acts = bell_draw(own_keys[0], (CKPT, TOKENS, D), 1.0, 6.0, ((1, 16),))
    doc_grads = bell_draw(own_keys[1], (CKPT, TOKENS, F), 1.0, 6.0, ((1, 16),))
    doc_segments = jax.vmap(lambda own: jnp.searchsorted(jnp.cumsum(uneven_parts(own, DOCS_DEV, TOK_DEV, SEG_MOST, 0)), jnp.arange(TOK_DEV), side="right"))(jax.random.split(own_keys[2], N_DOCS)).reshape((N_DOCS, TOK_DEV)).astype(jnp.int32)
    query_acts = bell_draw(own_keys[3], (CKPT, QTOKENS, D), 1.0, 6.0, ((1, 16),))
    query_grads = bell_draw(own_keys[4], (CKPT, QTOKENS, F), 1.0, 6.0, ((1, 16),))
    query_segments = jax.vmap(lambda own: jnp.searchsorted(jnp.cumsum(uneven_parts(own, Q_DEV, QTOK_DEV, 24, 0)), jnp.arange(QTOK_DEV), side="right"))(jax.random.split(own_keys[5], N_DOCS)).reshape((N_DOCS, QTOK_DEV)).astype(jnp.int32)
    input_proj = bell_draw(key_list[6], (D, K), D ** -0.5, 0.09375)
    output_proj = bell_draw(key_list[7], (F, K), F ** -0.5, 0.0546875)
    step_rates = jnp.clip(jnp.exp(jax.random.uniform(key_list[8], (CKPT,), jnp.float32, math.log(0.5), math.log(2.0))), 0.5, 2.0)
    return dict(doc_acts=doc_acts, doc_grads=doc_grads, doc_segments=doc_segments, query_acts=query_acts, query_grads=query_grads, query_segments=query_segments, input_proj=input_proj, output_proj=output_proj, step_rates=step_rates)


def shard_features(activ, gradient, segment_row, input_proj, output_proj, count):
    left_proj = jnp.dot(activ, input_proj, preferred_element_type=jnp.float32).astype(jnp.bfloat16)
    right_proj = jnp.dot(gradient, output_proj, preferred_element_type=jnp.float32).astype(jnp.bfloat16)
    onehot = (segment_row[:, None] == jnp.arange(count, dtype=jnp.int32)[None, :]).astype(left_proj.dtype)
    spread = (onehot[:, :, None] * left_proj[:, None, :]).reshape(activ.shape[0], count * K)
    summed = lax.dot_general(spread, right_proj, (((0,), (0,)), ((), ())), preferred_element_type=jnp.float32)
    return summed.reshape(count, K * K)


def all_features(activ_all, gradient_all, segments, input_proj, output_proj, rows, count, step_rates, scaled):
    columns = []
    for checkpoint in range(CKPT):
        activ = activ_all[checkpoint].reshape(N_DOCS, rows, D)
        gradient = gradient_all[checkpoint].reshape(N_DOCS, rows, F)
        blocks = lax.map(lambda items: shard_features(items[0], items[1], items[2], input_proj, output_proj, count), (activ, gradient, segments))
        blocks = blocks.reshape(N_DOCS * count, K * K)
        if scaled:
            blocks = (blocks * step_rates[checkpoint]).astype(jnp.bfloat16)
        columns.append(blocks)
    return jnp.concatenate(columns, axis=1)


def reference(doc_acts, doc_grads, doc_segments, query_acts, query_grads, query_segments, input_proj, output_proj, step_rates):
    doc_feat = all_features(doc_acts, doc_grads, doc_segments, input_proj, output_proj, TOK_DEV, DOCS_DEV, step_rates, True)
    query_feat = all_features(query_acts, query_grads, query_segments, input_proj, output_proj, QTOK_DEV, Q_DEV, step_rates, False)
    total = lax.dot_general(doc_feat.astype(jnp.float32), query_feat, (((1,), (1,)), ((), ())), precision=lax.Precision.HIGHEST, preferred_element_type=jnp.float32)
    return total * (4.0 / (K * K))
```

```python
import functools

import jax
import jax.numpy as jnp
from jax import lax
from jax.experimental import pallas as pl
from jax.experimental.pallas import tpu as pltpu
from jax.sharding import PartitionSpec as P

DOCS_DEV = 16
Q_DEV = 4
TAG = 16
MESH = pl.DeviceIdType.MESH
NT = (((1,), (1,)), ((), ()))


def cuts(extent, parts):
    units = extent // 256
    edges = [256 * (units * i // parts) for i in range(parts)] + [extent]
    return list(zip(edges[:-1], edges[1:]))


def flipped(value, mask):
    bit = 1
    while bit <= mask:
        if mask & bit:
            value = value + bit - 2 * bit * ((value // bit) % 2)
        bit *= 2
    return value


def kernel(
    outer,
    inner,
    act_cuts,
    grad_cuts,
    qa_hbm,
    qg_hbm,
    qs_hbm,
    da_hbm,
    dg_hbm,
    ds_hbm,
    wi_hbm,
    wo_hbm,
    rates_ref,
    out_ref,
    qa,
    qg,
    qs,
    da,
    dg,
    ds,
    wi,
    wo,
    lefts,
    rights,
    folded,
    load_sem,
    send_sem,
    recv_sem,
):
    me = lax.axis_index("docs")
    core, chip = me % 2, me // 2
    row, col = chip // inner, chip % inner
    n_pairs = outer * inner
    qtok = qs.shape[1]
    tok = ds.shape[1]

    def at(r, c, k):
        return (r * inner + c) * 2 + k

    loads = []

    def load(src, dst):
        copy = pltpu.make_async_copy(src, dst, load_sem.at[len(loads)])
        copy.start()
        loads.append(copy)
        return copy

    qs_load = load(qs_hbm, qs)
    wi_loads, qa_loads = [], []
    for a, b in act_cuts:
        wi_loads.append(load(wi_hbm.at[:, a:b], wi.at[:, a:b]))
        qa_loads.append(load(qa_hbm.at[:, :, a:b], qa.at[:, :, a:b]))
    wo_loads, qg_loads = [], []
    for a, b in grad_cuts:
        wo_loads.append(load(wo_hbm.at[:, a:b], wo.at[:, a:b]))
        qg_loads.append(load(qg_hbm.at[:, :, a:b], qg.at[:, :, a:b]))
    ds_load = load(ds_hbm, ds)
    da_loads = [load(da_hbm.at[:, :, a:b], da.at[:, :, a:b]) for a, b in act_cuts]
    dg_loads = [load(dg_hbm.at[:, :, a:b], dg.at[:, :, a:b]) for a, b in grad_cuts]

    rows_away = [flipped(row, i) for i in range(1, outer)]
    cols_away = [flipped(col, i) for i in range(1, inner)]
    peers = [at(r, col, core) for r in rows_away]
    peers += [at(row, c, core) for c in cols_away]
    peers += [at(row, col, 1 - core)]
    barrier = pltpu.get_barrier_semaphore()
    for peer in peers:
        pl.semaphore_signal(barrier, inc=1, device_id={"docs": peer}, device_id_type=MESH)

    sends = []

    def send(kind, slot, peer):
        block = (lefts, rights)[kind].at[slot]
        copy = pltpu.make_async_remote_copy(
            src_ref=block,
            dst_ref=block,
            send_sem=send_sem.at[len(sends)],
            recv_sem=recv_sem.at[kind, slot],
            device_id={"docs": peer},
            device_id_type=MESH,
        )
        copy.start()
        sends.append(copy)

    def arrived(kind, slot):
        block = (lefts, rights)[kind].at[slot]
        pltpu.make_async_remote_copy(
            src_ref=block,
            dst_ref=block,
            send_sem=send_sem.at[0],
            recv_sem=recv_sem.at[kind, slot],
            device_id={"docs": peers[-1]},
            device_id_type=MESH,
        ).wait_recv()

    def project(x, w, w_loads, x_loads, ranges):
        rows = x.shape[0] * x.shape[1]
        total = None
        for i, (a, b) in enumerate(ranges):
            if w_loads is not None:
                w_loads[i].wait()
            x_loads[i].wait()
            part = lax.dot_general(
                x[:, :, a:b].reshape(rows, b - a), w[:, a:b], NT, preferred_element_type=jnp.float32
            )
            total = part if total is None else total + part
        return total

    def beside(total):
        half = total.shape[0] // 2
        return jnp.concatenate([total[:half], total[half:]], axis=1).astype(jnp.bfloat16)

    qs_load.wait()
    width = 2 * qtok
    doubled = jnp.concatenate([qs[...], qs[...]], axis=1)
    lane = lax.broadcasted_iota(jnp.int32, (TAG, width), 1)
    line = lax.broadcasted_iota(jnp.int32, (TAG, width), 0)
    mine = (line == doubled + (me % (TAG // Q_DEV)) * Q_DEV) & (lane // qtok == core)
    lefts[me, qtok:, :] = mine.astype(jnp.float32).astype(jnp.bfloat16)
    lefts[me, :qtok, :] = beside(project(qa, wi, wi_loads, qa_loads, act_cuts))
    pl.semaphore_wait(barrier, len(peers))
    for peer in peers:
        send(0, me, peer)
    rights[me, :, :] = beside(project(qg, wo, wo_loads, qg_loads, grad_cuts))
    for peer in peers:
        send(1, me, peer)

    def pass_rows(kind):
        for r in rows_away:
            slot = at(r, col, core)
            arrived(kind, slot)
            for c in cols_away:
                send(kind, slot, at(row, c, core))
            send(kind, slot, at(row, col, 1 - core))

    def pass_cols(kind):
        for c in cols_away:
            for r in [row] + rows_away:
                slot = at(r, c, core)
                arrived(kind, slot)
                send(kind, slot, at(row, col, 1 - core))

    def spread(total):
        half = total.shape[0] // 2
        zero = jnp.zeros((half, total.shape[1]), jnp.float32)
        top = jnp.concatenate([total[:half], zero], axis=1)
        low = jnp.concatenate([zero, total[half:]], axis=1)
        return jnp.concatenate([top, low], axis=0).astype(jnp.bfloat16)

    doc_left = spread(project(da, wi, None, da_loads, act_cuts))
    pass_rows(0)
    doc_right = spread(project(dg, wo, None, dg_loads, grad_cuts))
    pass_rows(1)
    pass_cols(0)
    pass_cols(1)
    ds_load.wait()
    of_doc = lax.broadcasted_iota(jnp.int32, (DOCS_DEV, tok), 0) == ds[...]
    of_doc = of_doc.astype(jnp.float32).astype(jnp.bfloat16)
    of_doc = jnp.concatenate([of_doc, of_doc], axis=1)

    def fold(pair):
        left = lefts[pl.ds(2 * pair, 2), :qtok, :].reshape(width, -1)
        right = rights[pl.ds(2 * pair, 2), :, :].reshape(width, -1)
        a = lax.dot_general(doc_left, left, NT, preferred_element_type=jnp.float32)
        b = lax.dot_general(doc_right, right, NT, preferred_element_type=jnp.float32)
        ab = a * b
        s = ab[:tok] * rates_ref[0] + ab[tok:] * rates_ref[1]
        high = s.astype(jnp.bfloat16)
        low = (s - high.astype(jnp.float32)).astype(jnp.bfloat16)
        folded[pair] = jnp.dot(
            of_doc, jnp.concatenate([high, low], axis=0), preferred_element_type=jnp.float32
        )

    for c in [col] + cols_away:
        for r in [row] + rows_away:
            slot = at(r, c, 1 - core)
            arrived(0, slot)
            arrived(1, slot)
            fold(r * inner + c)

    chips = TAG // Q_DEV // 2
    group = min(n_pairs, 16)
    for g in range(0, n_pairs, group):
        t = jnp.concatenate([folded[p] for p in range(g, g + group)], axis=1)
        high = t.astype(jnp.bfloat16)
        low = (t - high.astype(jnp.float32)).astype(jnp.bfloat16)
        zero = jnp.zeros((TAG, width), jnp.bfloat16)
        lines = []
        for first in range(g, g + group, chips):
            lines.append(
                jnp.concatenate(
                    [
                        lefts[2 * p, qtok:, :] + lefts[2 * p + 1, qtok:, :]
                        if first <= p < first + chips
                        else zero
                        for p in range(g, g + group)
                    ],
                    axis=1,
                )
            )
        of_query = jnp.concatenate(lines, axis=0)
        both = lax.dot_general(
            jnp.concatenate([high, low], axis=0), of_query, NT, preferred_element_type=jnp.float32
        )
        k = doc_left.shape[1] // 2
        out_ref[:, g * 2 * Q_DEV : (g + group) * 2 * Q_DEV] = (both[:DOCS_DEV] + both[DOCS_DEV:]) * (
            4.0 / (k * k)
        )

    for copy in sends:
        copy.wait_send()


def per_device(
    doc_acts,
    doc_grads,
    doc_segments,
    query_acts,
    query_grads,
    query_segments,
    input_proj,
    output_proj,
    step_rates,
):
    n = lax.axis_size("docs")
    chips = n // 2
    inner = 1
    while 4 * inner * inner <= chips and chips % (2 * inner) == 0:
        inner *= 2
    outer = chips // inner
    d, k = input_proj.shape
    f = output_proj.shape[0]
    qtok = query_segments.shape[1]
    act_cuts, grad_cuts = cuts(d, 2), cuts(f, 4)
    n_loads = 2 + 3 * len(act_cuts) + 3 * len(grad_cuts)
    n_sends = 2 * (outer * inner + (outer - 1) * inner + inner - 1 + 1)
    hbm = pl.BlockSpec(memory_space=pl.ANY)
    return pl.pallas_call(
        functools.partial(kernel, outer, inner, act_cuts, grad_cuts),
        out_shape=jax.ShapeDtypeStruct((DOCS_DEV, Q_DEV * n), jnp.float32),
        in_specs=[hbm] * 8 + [pl.BlockSpec(memory_space=pltpu.SMEM)],
        out_specs=pl.BlockSpec(memory_space=pltpu.VMEM),
        scratch_shapes=[
            pltpu.VMEM(query_acts.shape, jnp.bfloat16),
            pltpu.VMEM(query_grads.shape, jnp.bfloat16),
            pltpu.VMEM(query_segments.shape, jnp.int32),
            pltpu.VMEM(doc_acts.shape, jnp.bfloat16),
            pltpu.VMEM(doc_grads.shape, jnp.bfloat16),
            pltpu.VMEM(doc_segments.shape, jnp.int32),
            pltpu.VMEM((k, d), jnp.bfloat16),
            pltpu.VMEM((k, f), jnp.bfloat16),
            pltpu.VMEM((n, qtok + TAG, 2 * k), jnp.bfloat16),
            pltpu.VMEM((n, qtok, 2 * k), jnp.bfloat16),
            pltpu.VMEM((chips, DOCS_DEV, 2 * qtok), jnp.float32),
            pltpu.SemaphoreType.DMA((n_loads,)),
            pltpu.SemaphoreType.DMA((n_sends,)),
            pltpu.SemaphoreType.DMA((2, n)),
        ],
        compiler_params=pltpu.CompilerParams(
            collective_id=0, has_side_effects=True, vmem_limit_bytes=56 << 20
        ),
    )(
        query_acts,
        query_grads,
        query_segments,
        doc_acts,
        doc_grads,
        doc_segments,
        input_proj.T,
        output_proj.T,
        step_rates,
    )


def solution(mesh):
    return jax.shard_map(
        per_device,
        mesh=mesh,
        in_specs=(
            P(None, ("groups", "docs"), None),
            P(None, ("groups", "docs"), None),
            P(("groups", "docs"), None),
            P(None, ("groups", "docs"), None),
            P(None, ("groups", "docs"), None),
            P(("groups", "docs"), None),
            P(),
            P(),
            P(),
        ),
        out_specs=P(("groups", "docs"), None),
        check_vma=False,
    )
```

```python
import functools

import jax
import jax.numpy as jnp
from jax import lax
from jax.experimental import pallas as pl
from jax.experimental.pallas import tpu as pltpu
from jax.sharding import PartitionSpec as P

DOCS_DEV = 16
Q_DEV = 4
MESH = pl.DeviceIdType.MESH
NT = (((1,), (1,)), ((), ()))


def cuts(extent, parts):
    units = extent // 256
    edges = [256 * (units * i // parts) for i in range(parts)] + [extent]
    return list(zip(edges[:-1], edges[1:]))


def flipped(value, mask):
    bit = 1
    while bit <= mask:
        if mask & bit:
            value = value + bit - 2 * bit * ((value // bit) % 2)
        bit *= 2
    return value


def kernel(
    outer,
    inner,
    act_cuts,
    grad_cuts,
    qa_hbm,
    qg_hbm,
    qs_hbm,
    da_hbm,
    dg_hbm,
    ds_hbm,
    wi_hbm,
    wo_hbm,
    rates_ref,
    out_ref,
    qa,
    qg,
    qs,
    da,
    dg,
    ds,
    wi,
    wo,
    q_left,
    q_right,
    d_left,
    d_right,
    outgoing,
    result,
    load_sem,
    send_sem,
    recv_sem,
    pair_sem,
):
    me = lax.axis_index("docs")
    mates = 2 * inner
    row, mate = me // mates, me % mates
    col, core = mate // 2, mate % 2
    qtok = qs.shape[1]
    tok = ds.shape[1]
    tag = Q_DEV * mates
    width = 2 * qtok

    loads = []

    def load(src, dst):
        copy = pltpu.make_async_copy(src, dst, load_sem.at[len(loads)])
        copy.start()
        loads.append(copy)
        return copy

    qs_load, ds_load = load(qs_hbm, qs), load(ds_hbm, ds)
    wi_loads, qa_loads = [], []
    for a, b in act_cuts:
        wi_loads.append(load(wi_hbm.at[:, a:b], wi.at[:, a:b]))
        qa_loads.append(load(qa_hbm.at[:, :, a:b], qa.at[:, :, a:b]))
    wo_loads, qg_loads = [], []
    for a, b in grad_cuts:
        wo_loads.append(load(wo_hbm.at[:, a:b], wo.at[:, a:b]))
        qg_loads.append(load(qg_hbm.at[:, :, a:b], qg.at[:, :, a:b]))

    rows_away = [flipped(row, i) for i in range(1, outer)]
    cols_away = [flipped(col, i) for i in range(1, inner)]
    other = 1 - core

    def at(r, c, k):
        return (r * inner + c) * 2 + k

    places = [(r, c) for c in cols_away for r in rows_away] + [(r, col) for r in rows_away]
    places += [(row, c) for c in cols_away]
    peers = [at(r, c, core) for r, c in places]
    sibling = at(row, col, other)
    barrier = pltpu.get_barrier_semaphore()
    for peer in peers + [sibling]:
        pl.semaphore_signal(barrier, inc=1, device_id={"docs": peer}, device_id_type=MESH)

    sends = []

    def send(src, dst, sem, peer):
        copy = pltpu.make_async_remote_copy(
            src_ref=src,
            dst_ref=dst,
            send_sem=send_sem.at[len(sends)],
            recv_sem=sem,
            device_id={"docs": peer},
            device_id_type=MESH,
        )
        copy.start()
        sends.append(copy)

    def arrived(block, sem):
        pltpu.make_async_remote_copy(
            src_ref=block,
            dst_ref=block,
            send_sem=send_sem.at[0],
            recv_sem=sem,
            device_id={"docs": sibling},
            device_id_type=MESH,
        ).wait_recv()

    def spread(kind, blocks):
        own = blocks.at[col, row]
        for peer in peers:
            send(own, own, recv_sem.at[kind, col, row], peer)

    def share(kind, blocks):
        send(blocks.at[core], blocks.at[core], pair_sem.at[kind], sibling)

    def project(x, w, w_loads, x_loads, ranges):
        rows = x.shape[0] * x.shape[1]
        total = None
        for i, (a, b) in enumerate(ranges):
            if w_loads is not None:
                w_loads[i].wait()
            x_loads[i].wait()
            part = lax.dot_general(
                x[:, :, a:b].reshape(rows, b - a), w[:, a:b], NT, preferred_element_type=jnp.float32
            )
            total = part if total is None else total + part
        return total

    def beside(total):
        half = total.shape[0] // 2
        return jnp.concatenate([total[:half], total[half:]], axis=1).astype(jnp.bfloat16)

    qs_load.wait()
    doubled = jnp.concatenate([qs[...], qs[...]], axis=1)
    lane = lax.broadcasted_iota(jnp.int32, (tag, width), 1)
    line = lax.broadcasted_iota(jnp.int32, (tag, width), 0)
    mine = (line == doubled + mate * Q_DEV) & (lane // qtok == row % 2)
    q_left[col, row, qtok:, :] = mine.astype(jnp.float32).astype(jnp.bfloat16)
    q_left[col, row, :qtok, :] = beside(project(qa, wi, wi_loads, qa_loads, act_cuts))
    da_loads = [load(da_hbm.at[:, :, a:b], da.at[:, :, a:b]) for a, b in act_cuts]
    pl.semaphore_wait(barrier, len(peers) + 1)
    spread(0, q_left)
    half = project(qg, wo, wo_loads[:2], qg_loads[:2], grad_cuts[:2])
    dg_loads = [load(dg_hbm.at[:, :, a:b], dg.at[:, :, a:b]) for a, b in grad_cuts]
    q_right[col, row] = beside(half + project(qg, wo, wo_loads[2:], qg_loads[2:], grad_cuts[2:]))
    spread(1, q_right)

    ds_load.wait()
    of_doc = lax.broadcasted_iota(jnp.int32, (DOCS_DEV, tok), 0) == ds[...]
    d_left[core, tok:, :] = of_doc.astype(jnp.float32).astype(jnp.bfloat16)
    d_left[core, :tok, :] = beside(project(da, wi, None, da_loads, act_cuts))
    share(0, d_left)
    d_right[core] = beside(project(dg, wo, None, dg_loads, grad_cuts))
    share(1, d_right)

    def apart(block):
        lanes = lax.broadcasted_iota(jnp.int32, block.shape, 1)
        wide = block.astype(jnp.float32)
        first = lanes < block.shape[1] // 2
        both = [jnp.where(first, wide, 0.0), jnp.where(first, 0.0, wide)]
        return jnp.concatenate(both, axis=0).astype(jnp.bfloat16)

    def halves(x):
        high = x.astype(jnp.bfloat16)
        return [high, (x - high.astype(jnp.float32)).astype(jnp.bfloat16)]

    blank = jnp.zeros((tag, width), jnp.bfloat16)

    def scores(k, c):
        blocks = q_left[c]
        left = blocks[:, :qtok].reshape(outer * qtok, -1)
        right = q_right[c].reshape(outer * qtok, -1)
        of_query = jnp.concatenate(
            [
                jnp.concatenate(
                    [blocks[r, qtok:] if r // 2 == i else blank for i in range(outer // 2)], axis=1
                )
                for r in range(outer)
            ],
            axis=0,
        )
        a = lax.dot_general(apart(d_left[k, :tok]), left, NT, preferred_element_type=jnp.float32)
        b = lax.dot_general(apart(d_right[k]), right, NT, preferred_element_type=jnp.float32)
        ab = a * b
        s = ab[:tok] * rates_ref[0] + ab[tok:] * rates_ref[1]
        of = d_left[k, tok:]
        t = jnp.dot(
            jnp.concatenate([of, of], axis=1),
            jnp.concatenate(halves(s), axis=0),
            preferred_element_type=jnp.float32,
        )
        both = lax.dot_general(
            jnp.concatenate(halves(t), axis=0), of_query, NT, preferred_element_type=jnp.float32
        )
        return both[:DOCS_DEV] + both[DOCS_DEV:]

    total = theirs = None
    for c in [col] + cols_away:
        for r in [row] + rows_away if c is not col else rows_away:
            arrived(q_left.at[c, r], recv_sem.at[0, c, r])
            arrived(q_right.at[c, r], recv_sem.at[1, c, r])
        if theirs is None:
            arrived(d_left.at[other], pair_sem.at[0])
            arrived(d_right.at[other], pair_sem.at[1])
        part = scores(other, c)
        theirs = part if theirs is None else theirs + part
        if c is ([col] + cols_away)[-1]:
            outgoing[:, : theirs.shape[1]] = theirs
            send(outgoing, result, pair_sem.at[2], sibling)
        part = scores(core, c)
        total = part if total is None else total + part
    arrived(result, pair_sem.at[2])
    k = wi.shape[0]
    out_ref[...] = (total + result[:, : total.shape[1]]) * (4.0 / (k * k))

    for copy in sends:
        copy.wait_send()


def per_device(
    doc_acts,
    doc_grads,
    doc_segments,
    query_acts,
    query_grads,
    query_segments,
    input_proj,
    output_proj,
    step_rates,
):
    n = lax.axis_size("docs")
    mates = 2
    while mates * mates < n and n % (2 * mates) == 0:
        mates *= 2
    outer, inner = n // mates, mates // 2
    d, k = input_proj.shape
    f = output_proj.shape[0]
    qtok, tok = query_segments.shape[1], doc_segments.shape[1]
    act_cuts, grad_cuts = cuts(d, 2), cuts(f, 4)
    n_loads = 2 + 3 * len(act_cuts) + 3 * len(grad_cuts)
    n_sends = 2 * (outer * inner - 1) + 3
    wide = max(128, Q_DEV * n)
    hbm = pl.BlockSpec(memory_space=pl.ANY)
    return pl.pallas_call(
        functools.partial(kernel, outer, inner, act_cuts, grad_cuts),
        out_shape=jax.ShapeDtypeStruct((DOCS_DEV, Q_DEV * n), jnp.float32),
        in_specs=[hbm] * 8 + [pl.BlockSpec(memory_space=pltpu.SMEM)],
        out_specs=pl.BlockSpec(memory_space=pltpu.VMEM),
        scratch_shapes=[
            pltpu.VMEM(query_acts.shape, jnp.bfloat16),
            pltpu.VMEM(query_grads.shape, jnp.bfloat16),
            pltpu.VMEM(query_segments.shape, jnp.int32),
            pltpu.VMEM(doc_acts.shape, jnp.bfloat16),
            pltpu.VMEM(doc_grads.shape, jnp.bfloat16),
            pltpu.VMEM(doc_segments.shape, jnp.int32),
            pltpu.VMEM((k, d), jnp.bfloat16),
            pltpu.VMEM((k, f), jnp.bfloat16),
            pltpu.VMEM((inner, outer, qtok + Q_DEV * mates, 2 * k), jnp.bfloat16),
            pltpu.VMEM((inner, outer, qtok, 2 * k), jnp.bfloat16),
            pltpu.VMEM((2, tok + DOCS_DEV, 2 * k), jnp.bfloat16),
            pltpu.VMEM((2, tok, 2 * k), jnp.bfloat16),
            pltpu.VMEM((DOCS_DEV, wide), jnp.float32),
            pltpu.VMEM((DOCS_DEV, wide), jnp.float32),
            pltpu.SemaphoreType.DMA((n_loads,)),
            pltpu.SemaphoreType.DMA((n_sends,)),
            pltpu.SemaphoreType.DMA((2, inner, outer)),
            pltpu.SemaphoreType.DMA((3,)),
        ],
        compiler_params=pltpu.CompilerParams(
            collective_id=0, has_side_effects=True, vmem_limit_bytes=56 << 20
        ),
    )(
        query_acts,
        query_grads,
        query_segments,
        doc_acts,
        doc_grads,
        doc_segments,
        input_proj.T,
        output_proj.T,
        step_rates,
    )


def solution(mesh):
    return jax.shard_map(
        per_device,
        mesh=mesh,
        in_specs=(
            P(None, ("groups", "docs"), None),
            P(None, ("groups", "docs"), None),
            P(("groups", "docs"), None),
            P(None, ("groups", "docs"), None),
            P(None, ("groups", "docs"), None),
            P(("groups", "docs"), None),
            P(),
            P(),
            P(),
        ),
        out_specs=P(("groups", "docs"), None),
        check_vma=False,
    )
```

```python
import functools

import jax
import jax.numpy as jnp
from jax import lax
from jax.experimental import pallas as pl
from jax.experimental.pallas import tpu as pltpu
from jax.sharding import PartitionSpec as P

DOCS_DEV = 16
Q_DEV = 4
MESH = pl.DeviceIdType.MESH
NT = (((1,), (1,)), ((), ()))


def cuts(extent, parts):
    units = extent // 256
    edges = [256 * (units * i // parts) for i in range(parts)] + [extent]
    return list(zip(edges[:-1], edges[1:]))


def flipped(value, mask):
    bit = 1
    while bit <= mask:
        if mask & bit:
            value = value + bit - 2 * bit * ((value // bit) % 2)
        bit *= 2
    return value


def kernel(
    outer,
    inner,
    act_cuts,
    grad_cuts,
    qa_hbm,
    qg_hbm,
    qs_hbm,
    da_hbm,
    dg_hbm,
    ds_hbm,
    wi_hbm,
    wo_hbm,
    rates_hbm,
    out_ref,
    qa,
    qg,
    qs,
    da,
    dg,
    ds,
    wi,
    wo,
    rates,
    q_left,
    q_right,
    d_left,
    d_right,
    outgoing,
    result,
    load_sem,
    send_sem,
    recv_sem,
    pair_sem,
):
    me = lax.axis_index("docs")
    mates = 2 * inner
    row, mate = me // mates, me % mates
    col, core = mate // 2, mate % 2
    qtok = qs.shape[1]
    tok = ds.shape[1]
    tag = Q_DEV * mates
    width = 2 * qtok

    rows_away = [flipped(row, i) for i in range(1, outer)]
    cols_away = [flipped(col, i) for i in range(1, inner)]
    other = 1 - core

    def at(r, c, k):
        return (r * inner + c) * 2 + k

    places = [(r, c) for c in cols_away for r in rows_away] + [(r, col) for r in rows_away]
    places += [(row, c) for c in cols_away]
    peers = [at(r, c, core) for r, c in places]
    sibling = at(row, col, other)
    barrier = pltpu.get_barrier_semaphore()
    for peer in peers + [sibling]:
        pl.semaphore_signal(barrier, inc=1, device_id={"docs": peer}, device_id_type=MESH)

    loads = []

    def load(src, dst):
        copy = pltpu.make_async_copy(src, dst, load_sem.at[len(loads)])
        copy.start()
        loads.append(copy)
        return copy

    qs_load, ds_load = load(qs_hbm, qs), load(ds_hbm, ds)
    rates_load = load(rates_hbm, rates)
    wi_loads, qa_loads = [], []
    for a, b in act_cuts:
        wi_loads.append(load(wi_hbm.at[:, a:b], wi.at[:, a:b]))
        qa_loads.append(load(qa_hbm.at[:, :, a:b], qa.at[:, :, a:b]))
    wo_loads, qg_loads = [], []
    for a, b in grad_cuts:
        wo_loads.append(load(wo_hbm.at[:, a:b], wo.at[:, a:b]))
        qg_loads.append(load(qg_hbm.at[:, :, a:b], qg.at[:, :, a:b]))

    sends = []

    def send(src, dst, sem, peer):
        copy = pltpu.make_async_remote_copy(
            src_ref=src,
            dst_ref=dst,
            send_sem=send_sem.at[len(sends)],
            recv_sem=sem,
            device_id={"docs": peer},
            device_id_type=MESH,
        )
        copy.start()
        sends.append(copy)

    def arrived(block, sem):
        pltpu.make_async_remote_copy(
            src_ref=block,
            dst_ref=block,
            send_sem=send_sem.at[0],
            recv_sem=sem,
            device_id={"docs": sibling},
            device_id_type=MESH,
        ).wait_recv()

    def spread(kind, blocks, away):
        own = blocks.at[col, row]
        for r, c in away:
            send(own, own, recv_sem.at[kind, col, row], at(r, c, core))

    def relay(kind, blocks):
        for r in rows_away:
            block = blocks.at[col, r]
            arrived(block, recv_sem.at[kind, col, r])
            for c in cols_away:
                send(block, block, recv_sem.at[kind, col, r], at(row, c, core))

    def share(kind, blocks):
        send(blocks.at[core], blocks.at[core], pair_sem.at[kind], sibling)

    def project(x, w, w_loads, x_loads, ranges):
        rows = x.shape[0] * x.shape[1]
        total = None
        for i, (a, b) in enumerate(ranges):
            if w_loads is not None:
                w_loads[i].wait()
            x_loads[i].wait()
            part = lax.dot_general(
                x[:, :, a:b].reshape(rows, b - a), w[:, a:b], NT, preferred_element_type=jnp.float32
            )
            total = part if total is None else total + part
        return total

    def beside(total):
        half = total.shape[0] // 2
        return jnp.concatenate([total[:half], total[half:]], axis=1).astype(jnp.bfloat16)

    qs_load.wait()
    doubled = jnp.concatenate([qs[...], qs[...]], axis=1)
    lane = lax.broadcasted_iota(jnp.int32, (tag, width), 1)
    line = lax.broadcasted_iota(jnp.int32, (tag, width), 0)
    mine = (line == doubled + mate * Q_DEV) & (lane // qtok == row % 2)
    q_left[col, row, qtok:, :] = mine.astype(jnp.float32).astype(jnp.bfloat16)
    q_left[col, row, :qtok, :] = beside(project(qa, wi, wi_loads, qa_loads, act_cuts))
    da_loads = [load(da_hbm.at[:, :, a:b], da.at[:, :, a:b]) for a, b in act_cuts]
    pl.semaphore_wait(barrier, len(peers) + 1)
    spread(0, q_left, places[len(cols_away) * len(rows_away) :])
    half = project(qg, wo, wo_loads[:2], qg_loads[:2], grad_cuts[:2])
    dg_loads = [load(dg_hbm.at[:, :, a:b], dg.at[:, :, a:b]) for a, b in grad_cuts]
    q_right[col, row] = beside(half + project(qg, wo, wo_loads[2:], qg_loads[2:], grad_cuts[2:]))
    spread(1, q_right, places)

    ds_load.wait()
    rates_load.wait()
    of_doc = lax.broadcasted_iota(jnp.int32, (DOCS_DEV, tok), 0) == ds[...]
    d_left[core, tok:, :] = of_doc.astype(jnp.float32).astype(jnp.bfloat16)
    d_left[core, :tok, :] = beside(project(da, wi, None, da_loads, act_cuts))
    share(0, d_left)
    half = project(dg, wo, None, dg_loads[:2], grad_cuts[:2])
    relay(0, q_left)
    d_right[core] = beside(half + project(dg, wo, None, dg_loads[2:], grad_cuts[2:]))
    share(1, d_right)

    def apart(block):
        lanes = lax.broadcasted_iota(jnp.int32, block.shape, 1)
        wide = block.astype(jnp.float32)
        first = lanes < block.shape[1] // 2
        both = [jnp.where(first, wide, 0.0), jnp.where(first, 0.0, wide)]
        return jnp.concatenate(both, axis=0).astype(jnp.bfloat16)

    def halves(x):
        high = x.astype(jnp.bfloat16)
        return [high, (x - high.astype(jnp.float32)).astype(jnp.bfloat16)]

    blank = jnp.zeros((tag, width), jnp.bfloat16)

    def scores(k, c):
        blocks = q_left[c]
        left = blocks[:, :qtok].reshape(outer * qtok, -1)
        right = q_right[c].reshape(outer * qtok, -1)
        of_query = jnp.concatenate(
            [
                jnp.concatenate(
                    [blocks[r, qtok:] if r // 2 == i else blank for i in range(outer // 2)], axis=1
                )
                for r in range(outer)
            ],
            axis=0,
        )
        a = lax.dot_general(apart(d_left[k, :tok]), left, NT, preferred_element_type=jnp.float32)
        b = lax.dot_general(apart(d_right[k]), right, NT, preferred_element_type=jnp.float32)
        ab = a * b
        s = ab[:tok] * rates[0] + ab[tok:] * rates[1]
        of = d_left[k, tok:]
        t = jnp.dot(
            jnp.concatenate([of, of], axis=1),
            jnp.concatenate(halves(s), axis=0),
            preferred_element_type=jnp.float32,
        )
        both = lax.dot_general(
            jnp.concatenate(halves(t), axis=0), of_query, NT, preferred_element_type=jnp.float32
        )
        return both[:DOCS_DEV] + both[DOCS_DEV:]

    total = theirs = None
    for c in [col] + cols_away:
        for r in [row] + rows_away if c is not col else rows_away:
            if c is not col:
                arrived(q_left.at[c, r], recv_sem.at[0, c, r])
            arrived(q_right.at[c, r], recv_sem.at[1, c, r])
        if total is None:
            total = scores(core, c)
            arrived(d_left.at[other], pair_sem.at[0])
            arrived(d_right.at[other], pair_sem.at[1])
            theirs = scores(other, c)
        else:
            theirs = theirs + scores(other, c)
        if c is ([col] + cols_away)[-1]:
            outgoing[:, : theirs.shape[1]] = theirs
            send(outgoing, result, pair_sem.at[2], sibling)
        if c is not col:
            total = total + scores(core, c)
    arrived(result, pair_sem.at[2])
    k = wi.shape[0]
    out_ref[...] = (total + result[:, : total.shape[1]]) * (4.0 / (k * k))

    for copy in sends:
        copy.wait_send()


def per_device(
    doc_acts,
    doc_grads,
    doc_segments,
    query_acts,
    query_grads,
    query_segments,
    input_proj,
    output_proj,
    step_rates,
):
    n = lax.axis_size("docs")
    mates = 2
    while mates * mates < n and n % (2 * mates) == 0:
        mates *= 2
    outer, inner = n // mates, mates // 2
    d, k = input_proj.shape
    f = output_proj.shape[0]
    qtok, tok = query_segments.shape[1], doc_segments.shape[1]
    act_cuts, grad_cuts = cuts(d, 1), cuts(f, 4)
    n_loads = 3 + 3 * len(act_cuts) + 3 * len(grad_cuts)
    n_sends = 2 * (outer * inner - 1) + 3
    wide = max(128, Q_DEV * n)
    hbm = pl.BlockSpec(memory_space=pl.ANY)
    return pl.pallas_call(
        functools.partial(kernel, outer, inner, act_cuts, grad_cuts),
        out_shape=jax.ShapeDtypeStruct((DOCS_DEV, Q_DEV * n), jnp.float32),
        in_specs=[hbm] * 9,
        out_specs=pl.BlockSpec(memory_space=pltpu.VMEM),
        scratch_shapes=[
            pltpu.VMEM(query_acts.shape, jnp.bfloat16),
            pltpu.VMEM(query_grads.shape, jnp.bfloat16),
            pltpu.VMEM(query_segments.shape, jnp.int32),
            pltpu.VMEM(doc_acts.shape, jnp.bfloat16),
            pltpu.VMEM(doc_grads.shape, jnp.bfloat16),
            pltpu.VMEM(doc_segments.shape, jnp.int32),
            pltpu.VMEM((k, d), jnp.bfloat16),
            pltpu.VMEM((k, f), jnp.bfloat16),
            pltpu.SMEM(step_rates.shape, jnp.float32),
            pltpu.VMEM((inner, outer, qtok + Q_DEV * mates, 2 * k), jnp.bfloat16),
            pltpu.VMEM((inner, outer, qtok, 2 * k), jnp.bfloat16),
            pltpu.VMEM((2, tok + DOCS_DEV, 2 * k), jnp.bfloat16),
            pltpu.VMEM((2, tok, 2 * k), jnp.bfloat16),
            pltpu.VMEM((DOCS_DEV, wide), jnp.float32),
            pltpu.VMEM((DOCS_DEV, wide), jnp.float32),
            pltpu.SemaphoreType.DMA((n_loads,)),
            pltpu.SemaphoreType.DMA((n_sends,)),
            pltpu.SemaphoreType.DMA((2, inner, outer)),
            pltpu.SemaphoreType.DMA((3,)),
        ],
        compiler_params=pltpu.CompilerParams(
            collective_id=0, has_side_effects=True, vmem_limit_bytes=56 << 20
        ),
    )(
        query_acts,
        query_grads,
        query_segments,
        doc_acts,
        doc_grads,
        doc_segments,
        input_proj.T,
        output_proj.T,
        step_rates,
    )


def solution(mesh):
    return jax.shard_map(
        per_device,
        mesh=mesh,
        in_specs=(
            P(None, ("groups", "docs"), None),
            P(None, ("groups", "docs"), None),
            P(("groups", "docs"), None),
            P(None, ("groups", "docs"), None),
            P(None, ("groups", "docs"), None),
            P(("groups", "docs"), None),
            P(),
            P(),
            P(),
        ),
        out_specs=P(("groups", "docs"), None),
        check_vma=False,
    )
```

```python
import functools

import jax
import jax.numpy as jnp
from jax import lax
from jax.experimental import pallas as pl
from jax.experimental.pallas import tpu as pltpu
from jax.sharding import PartitionSpec as P

DOCS_DEV = 16
Q_DEV = 4
MESH = pl.DeviceIdType.MESH
NT = (((1,), (1,)), ((), ()))


def cuts(extent, parts):
    units = extent // 256
    edges = [256 * (units * i // parts) for i in range(parts)] + [extent]
    return list(zip(edges[:-1], edges[1:]))


def flipped(value, mask):
    bit = 1
    while bit <= mask:
        if mask & bit:
            value = value + bit - 2 * bit * ((value // bit) % 2)
        bit *= 2
    return value


def kernel(
    outer,
    inner,
    act_cuts,
    grad_cuts,
    qa_hbm,
    qg_hbm,
    qs_hbm,
    da_hbm,
    dg_hbm,
    ds_hbm,
    wi_hbm,
    wo_hbm,
    rates_hbm,
    out_ref,
    qa,
    qg,
    qs,
    da,
    dg,
    ds,
    wi,
    wo,
    rates,
    q_left,
    q_right,
    d_left,
    d_right,
    outgoing,
    result,
    load_sem,
    send_sem,
    recv_sem,
    pair_sem,
):
    me = lax.axis_index("docs")
    mates = 2 * inner
    row, mate = me // mates, me % mates
    col, core = mate // 2, mate % 2
    qtok = qs.shape[1]
    tok = ds.shape[1]
    tag = Q_DEV * mates
    width = 2 * qtok

    rows_away = [flipped(row, i) for i in range(1, outer)]
    cols_away = [flipped(col, i) for i in range(1, inner)]
    other = 1 - core

    def at(r, c, k):
        return (r * inner + c) * 2 + k

    places = [(r, c) for c in cols_away for r in rows_away] + [(r, col) for r in rows_away]
    places += [(row, c) for c in cols_away]
    peers = [at(r, c, core) for r, c in places]
    sibling = at(row, col, other)
    barrier = pltpu.get_barrier_semaphore()
    for peer in peers + [sibling]:
        pl.semaphore_signal(barrier, inc=1, device_id={"docs": peer}, device_id_type=MESH)

    loads = []

    def load(src, dst):
        copy = pltpu.make_async_copy(src, dst, load_sem.at[len(loads)])
        copy.start()
        loads.append(copy)
        return copy

    qs_load, ds_load = load(qs_hbm, qs), load(ds_hbm, ds)
    rates_load = load(rates_hbm, rates)
    wi_loads, qa_loads = [], []
    for a, b in act_cuts:
        wi_loads.append(load(wi_hbm.at[:, a:b], wi.at[:, a:b]))
        qa_loads.append(load(qa_hbm.at[:, :, a:b], qa.at[:, :, a:b]))
    wo_loads, qg_loads = [], []
    for a, b in grad_cuts:
        wo_loads.append(load(wo_hbm.at[:, a:b], wo.at[:, a:b]))
        qg_loads.append(load(qg_hbm.at[:, :, a:b], qg.at[:, :, a:b]))

    sends = []

    def send(src, dst, sem, peer):
        copy = pltpu.make_async_remote_copy(
            src_ref=src,
            dst_ref=dst,
            send_sem=send_sem.at[len(sends)],
            recv_sem=sem,
            device_id={"docs": peer},
            device_id_type=MESH,
        )
        copy.start()
        sends.append(copy)

    def arrived(block, sem):
        pltpu.make_async_remote_copy(
            src_ref=block,
            dst_ref=block,
            send_sem=send_sem.at[0],
            recv_sem=sem,
            device_id={"docs": sibling},
            device_id_type=MESH,
        ).wait_recv()

    def spread(kind, blocks, away):
        own = blocks.at[col, row]
        for r, c in away:
            send(own, own, recv_sem.at[kind, col, row], at(r, c, core))

    def relay(kind, blocks):
        for r in rows_away:
            block = blocks.at[col, r]
            arrived(block, recv_sem.at[kind, col, r])
            for c in cols_away:
                send(block, block, recv_sem.at[kind, col, r], at(row, c, core))

    def share(kind, blocks):
        send(blocks.at[core], blocks.at[core], pair_sem.at[kind], sibling)

    def project(x, w, w_loads, x_loads, ranges):
        rows = x.shape[0] * x.shape[1]
        total = None
        for i, (a, b) in enumerate(ranges):
            if w_loads is not None:
                w_loads[i].wait()
            x_loads[i].wait()
            part = lax.dot_general(
                x[:, :, a:b].reshape(rows, b - a), w[:, a:b], NT, preferred_element_type=jnp.float32
            )
            total = part if total is None else total + part
        return total

    def beside(total):
        half = total.shape[0] // 2
        return jnp.concatenate([total[:half], total[half:]], axis=1).astype(jnp.bfloat16)

    qs_load.wait()
    doubled = jnp.concatenate([qs[...], qs[...]], axis=1)
    lane = lax.broadcasted_iota(jnp.int32, (tag, width), 1)
    line = lax.broadcasted_iota(jnp.int32, (tag, width), 0)
    mine = (line == doubled + mate * Q_DEV) & (lane // qtok == row % 2)
    q_left[col, row, qtok:, :] = mine.astype(jnp.float32).astype(jnp.bfloat16)
    q_left[col, row, :qtok, :] = beside(project(qa, wi, wi_loads, qa_loads, act_cuts))
    da_loads = [load(da_hbm.at[:, :, a:b], da.at[:, :, a:b]) for a, b in act_cuts]
    pl.semaphore_wait(barrier, len(peers) + 1)
    spread(0, q_left, places[len(cols_away) * len(rows_away) :])
    half = project(qg, wo, wo_loads[:1], qg_loads[:1], grad_cuts[:1])
    dg_loads = [load(dg_hbm.at[:, :, a:b], dg.at[:, :, a:b]) for a, b in grad_cuts]
    q_right[col, row] = beside(half + project(qg, wo, wo_loads[1:], qg_loads[1:], grad_cuts[1:]))
    spread(1, q_right, places)

    ds_load.wait()
    rates_load.wait()
    of_doc = lax.broadcasted_iota(jnp.int32, (DOCS_DEV, tok), 0) == ds[...]
    d_left[core, tok:, :] = of_doc.astype(jnp.float32).astype(jnp.bfloat16)
    d_left[core, :tok, :] = beside(project(da, wi, None, da_loads, act_cuts))
    share(0, d_left)
    half = project(dg, wo, None, dg_loads[:1], grad_cuts[:1])
    relay(0, q_left)
    d_right[core] = beside(half + project(dg, wo, None, dg_loads[1:], grad_cuts[1:]))
    share(1, d_right)

    def apart(block):
        lanes = lax.broadcasted_iota(jnp.int32, block.shape, 1)
        wide = block.astype(jnp.float32)
        first = lanes < block.shape[1] // 2
        both = [jnp.where(first, wide, 0.0), jnp.where(first, 0.0, wide)]
        return jnp.concatenate(both, axis=0).astype(jnp.bfloat16)

    def halves(x):
        high = x.astype(jnp.bfloat16)
        return [high, (x - high.astype(jnp.float32)).astype(jnp.bfloat16)]

    blank = jnp.zeros((tag, width), jnp.bfloat16)

    def scores(k, c):
        blocks = q_left[c]
        left = blocks[:, :qtok].reshape(outer * qtok, -1)
        right = q_right[c].reshape(outer * qtok, -1)
        of_query = jnp.concatenate(
            [
                jnp.concatenate(
                    [blocks[r, qtok:] if r // 2 == i else blank for i in range(outer // 2)], axis=1
                )
                for r in range(outer)
            ],
            axis=0,
        )
        a = lax.dot_general(apart(d_left[k, :tok]), left, NT, preferred_element_type=jnp.float32)
        b = lax.dot_general(apart(d_right[k]), right, NT, preferred_element_type=jnp.float32)
        ab = a * b
        s = ab[:tok] * rates[0] + ab[tok:] * rates[1]
        of = d_left[k, tok:]
        t = jnp.dot(
            jnp.concatenate([of, of], axis=1),
            jnp.concatenate(halves(s), axis=0),
            preferred_element_type=jnp.float32,
        )
        both = lax.dot_general(
            jnp.concatenate(halves(t), axis=0), of_query, NT, preferred_element_type=jnp.float32
        )
        return both[:DOCS_DEV] + both[DOCS_DEV:]

    total = theirs = None
    for c in [col] + cols_away:
        for r in [row] + rows_away if c is not col else rows_away:
            if c is not col:
                arrived(q_left.at[c, r], recv_sem.at[0, c, r])
            arrived(q_right.at[c, r], recv_sem.at[1, c, r])
        if total is None:
            total = scores(core, c)
            arrived(d_left.at[other], pair_sem.at[0])
            arrived(d_right.at[other], pair_sem.at[1])
            theirs = scores(other, c)
        else:
            theirs = theirs + scores(other, c)
        if c is ([col] + cols_away)[-1]:
            outgoing[:, : theirs.shape[1]] = theirs
            send(outgoing, result, pair_sem.at[2], sibling)
        if c is not col:
            total = total + scores(core, c)
    arrived(result, pair_sem.at[2])
    k = wi.shape[0]
    out_ref[...] = (total + result[:, : total.shape[1]]) * (4.0 / (k * k))

    for copy in sends:
        copy.wait_send()


def per_device(
    doc_acts,
    doc_grads,
    doc_segments,
    query_acts,
    query_grads,
    query_segments,
    input_proj,
    output_proj,
    step_rates,
):
    n = lax.axis_size("docs")
    mates = 2
    while mates * mates < n and n % (2 * mates) == 0:
        mates *= 2
    outer, inner = n // mates, mates // 2
    d, k = input_proj.shape
    f = output_proj.shape[0]
    qtok, tok = query_segments.shape[1], doc_segments.shape[1]
    act_cuts, grad_cuts = cuts(d, 1), cuts(f, 2)
    n_loads = 3 + 3 * len(act_cuts) + 3 * len(grad_cuts)
    n_sends = 2 * (outer * inner - 1) + 3
    wide = max(128, Q_DEV * n)
    hbm = pl.BlockSpec(memory_space=pl.ANY)
    return pl.pallas_call(
        functools.partial(kernel, outer, inner, act_cuts, grad_cuts),
        out_shape=jax.ShapeDtypeStruct((DOCS_DEV, Q_DEV * n), jnp.float32),
        in_specs=[hbm] * 9,
        out_specs=pl.BlockSpec(memory_space=pltpu.VMEM),
        scratch_shapes=[
            pltpu.VMEM(query_acts.shape, jnp.bfloat16),
            pltpu.VMEM(query_grads.shape, jnp.bfloat16),
            pltpu.VMEM(query_segments.shape, jnp.int32),
            pltpu.VMEM(doc_acts.shape, jnp.bfloat16),
            pltpu.VMEM(doc_grads.shape, jnp.bfloat16),
            pltpu.VMEM(doc_segments.shape, jnp.int32),
            pltpu.VMEM((k, d), jnp.bfloat16),
            pltpu.VMEM((k, f), jnp.bfloat16),
            pltpu.SMEM(step_rates.shape, jnp.float32),
            pltpu.VMEM((inner, outer, qtok + Q_DEV * mates, 2 * k), jnp.bfloat16),
            pltpu.VMEM((inner, outer, qtok, 2 * k), jnp.bfloat16),
            pltpu.VMEM((2, tok + DOCS_DEV, 2 * k), jnp.bfloat16),
            pltpu.VMEM((2, tok, 2 * k), jnp.bfloat16),
            pltpu.VMEM((DOCS_DEV, wide), jnp.float32),
            pltpu.VMEM((DOCS_DEV, wide), jnp.float32),
            pltpu.SemaphoreType.DMA((n_loads,)),
            pltpu.SemaphoreType.DMA((n_sends,)),
            pltpu.SemaphoreType.DMA((2, inner, outer)),
            pltpu.SemaphoreType.DMA((3,)),
        ],
        compiler_params=pltpu.CompilerParams(
            collective_id=0, has_side_effects=True, vmem_limit_bytes=56 << 20
        ),
    )(
        query_acts,
        query_grads,
        query_segments,
        doc_acts,
        doc_grads,
        doc_segments,
        input_proj.T,
        output_proj.T,
        step_rates,
    )


def solution(mesh):
    return jax.shard_map(
        per_device,
        mesh=mesh,
        in_specs=(
            P(None, ("groups", "docs"), None),
            P(None, ("groups", "docs"), None),
            P(("groups", "docs"), None),
            P(None, ("groups", "docs"), None),
            P(None, ("groups", "docs"), None),
            P(("groups", "docs"), None),
            P(),
            P(),
            P(),
        ),
        out_specs=P(("groups", "docs"), None),
        check_vma=False,
    )
```
